256 devices in a mesh: row: 16 (over y_lo, x, core), col: 16 (over z, y_hi).
Axes of the slice: x: 4, y: 4 (y_hi: 2, y_lo: 2; y = y_hi * 2 + y_lo), z: 8, core: 2. Of those that a mesh axis runs over, the one named last changes fastest.
Arguments:
- pair_act: bfloat16 [512, 512, 128], P('row', 'col'), may hold values from -6 to 6
- out_grad: bfloat16 [512, 512, 128], P('row', 'col'), may hold values from -6 to 6
- valid_count: int32 [1], replicated, may hold values from 128 to 511
- w_in: bfloat16 [128, 640], replicated, may hold values from -0.5 to 0.5
- w_out: bfloat16 [128, 128], replicated, may hold values from -0.5 to 0.5
- in_gain: float32 [128], replicated, may hold values from 0.5 to 1.5
- in_bias: float32 [128], replicated, may hold values from -3 to 3
- out_gain: float32 [128], replicated, may hold values from 0.5 to 1.5
- out_bias: float32 [128], replicated, may hold values from -3 to 3
Outputs:
- grad_pair: bfloat16 [512, 512, 128], P('row', 'col')
- grad_in: float32 [128, 640], replicated
- grad_out: float32 [128, 128], replicated
The draws below stay inside these ranges and needn't reach their ends.
All inputs are finite; a program needn't handle non-finite values.
Results may differ from the reference program's by a relative error of at most 0.02.
Values may be sent and summed in bfloat16 or wider, within the bound.
No kernel may reach another device: no remote copies, remote signals or barrier semaphores. Data moves between devices by JAX's collectives and lax.ppermute only.
A program may use at most 128 MiB of HBM per device.

```python
import jax
import jax.numpy as jnp
from jax import lax

C = 128
HIDDEN_SIZE = 128
TOKENS = 512


def shard_levels(rng, dims, pieces, least, high):
    def one(dim, blocks):
        steps = jax.random.uniform(jax.random.fold_in(jax.random.fold_in(rng, 6), dim), (blocks,), jnp.float32, least / len(pieces), high / len(pieces))
        return jnp.repeat(jnp.exp(steps), dims[dim] // blocks).reshape((-1,) + (1,) * (len(dims) - dim - 1))

    level = one(*pieces[0])
    for cut in pieces[1:]:
        level = level * one(*cut)
    return level


def noise(stream_key, dims, spread, bound, pieces=(), held_as=jnp.bfloat16):
    level = shard_levels(stream_key, dims, pieces, -0.22, 0.18) if pieces else 1.0
    values = jax.random.normal(stream_key, dims, jnp.float32) * spread * level
    return jnp.minimum(jnp.maximum(values, -bound), bound).astype(held_as)


def setup_inputs(seed: int = 0) -> dict:
    seeds = jax.random.split(jax.random.key(seed), 10)
    pair_act = noise(seeds[0], (TOKENS, TOKENS, C), 1.0, 6.0, ((0, 16), (1, 16)))
    out_grad = noise(seeds[1], (TOKENS, TOKENS, C), 1.0, 6.0, ((0, 16), (1, 16)))
    valid_count = jax.random.randint(seeds[2], (1,), TOKENS // 4, TOKENS).astype(jnp.int32)
    w_in = noise(seeds[3], (C, 4 * HIDDEN_SIZE + C), C ** -0.5, 0.5)
    w_out = noise(seeds[4], (HIDDEN_SIZE, C), HIDDEN_SIZE ** -0.5, 0.5)
    in_gain = jnp.clip(1.0 + 0.1 * jax.random.normal(seeds[5], (C,), jnp.float32), 0.5, 1.5)
    in_bias = noise(seeds[6], (C,), 0.5, 3.0, (), jnp.float32)
    out_gain = jnp.clip(1.0 + 0.1 * jax.random.normal(seeds[7], (HIDDEN_SIZE,), jnp.float32), 0.5, 1.5)
    out_bias = noise(seeds[8], (HIDDEN_SIZE,), 0.5, 3.0, (), jnp.float32)
    return {"pair_act": pair_act, "out_grad": out_grad, "valid_count": valid_count, "w_in": w_in, "w_out": w_out, "in_gain": in_gain, "in_bias": in_bias, "out_gain": out_gain, "out_bias": out_bias}


EPS = 1e-05

def norm_forward(values, gain, bias):
    mean = lax.optimization_barrier(jnp.mean(values, axis=-1, keepdims=True))
    centred = values - mean
    rstd = lax.rsqrt(lax.optimization_barrier(jnp.mean(centred * centred, axis=-1, keepdims=True)) + EPS)
    unit = centred * rstd
    return (unit * gain + bias, unit, rstd)

def norm_backward(grad, unit, rstd, gain):
    scaled = grad * gain
    first = lax.optimization_barrier(jnp.mean(scaled, axis=-1, keepdims=True))
    second = lax.optimization_barrier(jnp.mean(scaled * unit, axis=-1, keepdims=True))
    return rstd * (scaled - first - unit * second)

def reference(pair_act, out_grad, valid_count, w_in, w_out, in_gain, in_bias, out_gain, out_bias):
    f32 = jnp.float32
    bf16 = jnp.bfloat16
    hidden = w_out.shape[0]
    valid = (jnp.arange(TOKENS) < valid_count[0]).astype(f32)
    both = valid[:, None, None] * valid[None, :, None]
    normed, z_unit, z_rstd = norm_forward(pair_act.astype(f32), in_gain, in_bias)
    normed16 = normed.astype(bf16)
    proj = jnp.einsum('ijc,cd->ijd', normed16.astype(f32), w_in.astype(f32))
    left_val = proj[..., :hidden]
    left_sig = jax.nn.sigmoid(proj[..., hidden:2 * hidden])
    right_val = proj[..., 2 * hidden:3 * hidden]
    right_sig = jax.nn.sigmoid(proj[..., 3 * hidden:4 * hidden])
    gate = jax.nn.sigmoid(proj[..., 4 * hidden:])
    left16 = (left_sig * left_val * both).astype(bf16)
    right16 = (right_sig * right_val * both).astype(bf16)
    tri = jnp.einsum('ikh,jkh->ijh', left16.astype(f32), right16.astype(f32))
    tri_norm, tri_unit, tri_rstd = norm_forward(tri, out_gain, out_bias)
    tri16 = tri_norm.astype(bf16)
    projected = jnp.einsum('ijh,hc->ijc', tri16.astype(f32), w_out.astype(f32))
    cotangent = out_grad.astype(f32)
    scaled16 = (cotangent * gate).astype(bf16)
    gate_grad = cotangent * projected * gate * (1.0 - gate)
    grad_out = jnp.einsum('ijh,ijc->hc', tri16.astype(f32), scaled16.astype(f32)) / TOKENS
    tri_back = jnp.einsum('ijc,hc->ijh', scaled16.astype(f32), w_out.astype(f32))
    tri_grad16 = norm_backward(tri_back, tri_unit, tri_rstd, out_gain).astype(bf16)
    left_grad = jnp.einsum('ijh,jkh->ikh', tri_grad16.astype(f32), right16.astype(f32))
    right_grad = jnp.einsum('ijh,ikh->jkh', tri_grad16.astype(f32), left16.astype(f32))
    proj_grad16 = jnp.concatenate([left_grad * both * left_sig, left_grad * both * left_val * left_sig * (1.0 - left_sig), right_grad * both * right_sig, right_grad * both * right_val * right_sig * (1.0 - right_sig), gate_grad], axis=-1).astype(bf16)
    grad_in = jnp.einsum('ijc,ijd->cd', normed16.astype(f32), proj_grad16.astype(f32)) / TOKENS
    normed_grad = jnp.einsum('ijd,cd->ijc', proj_grad16.astype(f32), w_in.astype(f32))
    grad_pair = norm_backward(normed_grad, z_unit, z_rstd, in_gain).astype(bf16)
    return (grad_pair, grad_in, grad_out)
```

```python
import functools

import jax
import jax.numpy as jnp
from jax import lax
from jax.experimental import pallas as pl
from jax.experimental.pallas import tpu as pltpu
from jax.sharding import Mesh
from jax.sharding import PartitionSpec as P

EPS = 1e-05
F32 = jnp.float32
BF16 = jnp.bfloat16
ROW = ("rh", "core")
CHIPS = ("rh", "col")
VMEM = pl.BlockSpec(memory_space=pltpu.VMEM)
SMEM = pl.BlockSpec(memory_space=pltpu.SMEM)


def column(ref):
    wide = jnp.broadcast_to(ref[...], (128, 128)).T
    return jnp.concatenate([wide, wide], axis=1)


def dot(a, b, dims):
    return lax.dot_general(a, b, ((dims[:1], dims[1:]), ((), ())), preferred_element_type=F32)


def norm_unit(values):
    mean = jnp.sum(values, axis=0, keepdims=True) * (1.0 / 128)
    centred = values - mean
    var = jnp.sum(centred * centred, axis=0, keepdims=True) * (1.0 / 128)
    rstd = lax.rsqrt(var + EPS)
    return centred * rstd, rstd


def norm_backward(grad, unit, rstd, gain):
    scaled = grad * gain
    first = jnp.sum(scaled, axis=0, keepdims=True) * (1.0 / 128)
    second = jnp.sum(scaled * unit, axis=0, keepdims=True) * (1.0 / 128)
    return rstd * (scaled - first - unit * second)


def pair_mask(valid, n):
    lane = lax.broadcasted_iota(jnp.int32, (1, 256), 1)
    first = 8 * ((lane // 32) % 4) + 2 * n + lane // 128
    row = 32 * (2 * lax.axis_index("rh") + lax.axis_index("core")) + first
    col = 32 * lax.axis_index("col") + lane % 32
    return ((row < valid) & (col < valid)).astype(F32)


def load_t(ref, n):
    return jnp.concatenate(
        [ref[:, q].reshape(128, 128).astype(F32).T for q in (2 * n, 2 * n + 1)], axis=1
    )


def load_strided(ref, n, first, stride):
    return jnp.concatenate(
        [ref[pl.ds(first + q, 128, stride=stride), :] for q in (2 * n, 2 * n + 1)], axis=1
    )


def store_strided(ref, n, first, stride, values):
    for d in range(2):
        ref[pl.ds(first + 2 * n + d, 128, stride=stride), :] = values[:, 128 * d : 128 * d + 128]


def swap_groups(parts):
    lane = lax.broadcasted_iota(jnp.int32, parts[0].shape, 1)
    low, even = lane < 64, lane % 64 < 32
    mid = [None] * 4
    for f in range(2):
        x, y = parts[f], parts[f + 2]
        mid[f] = jnp.where(low, x, pltpu.roll(y, 64, 1))
        mid[f + 2] = jnp.where(low, pltpu.roll(x, 64, 1), y)
    out = [None] * 4
    for f in (0, 2):
        x, y = mid[f], mid[f + 1]
        out[f] = jnp.where(even, x, pltpu.roll(y, 32, 1))
        out[f + 1] = jnp.where(even, pltpu.roll(x, 96, 1), y)
    return out


def project_kernel(valid_ref, x_ref, w_ref, gain_ref, bias_ref, xt_ref, nt_ref, lr_ref, scr):
    gain, bias = column(gain_ref), column(bias_ref)
    for n in range(4):
        x = load_t(x_ref, n)
        lanes = slice(256 * n, 256 * n + 256)
        xt_ref[:, lanes] = x.astype(BF16)
        unit, _ = norm_unit(x)
        normed = (unit * gain + bias).astype(BF16)
        nt_ref[:, lanes] = normed
        proj = dot(w_ref[:, :512], normed, (0, 0))
        mask = pair_mask(valid_ref[0], n)
        left = jax.nn.sigmoid(proj[128:256]) * proj[:128] * mask
        right = jax.nn.sigmoid(proj[384:512]) * proj[256:384] * mask
        store_strided(scr, n, 0, 16, left)
        store_strided(scr, n, 8, 16, right)
    lr_ref[...] = scr[...].reshape(128, 16, 128).astype(BF16)


def triangle_kernel(own_ref, other_ref, mats_ref, tri_ref):
    me = lax.axis_index("core")
    for ref, core in ((own_ref, me), (other_ref, 1 - me)):
        for t in range(4):
            parts = [
                ref[:, 4 * t + f].astype(F32).reshape(128, 128) for f in range(4)
            ]
            rows = [y.reshape(8, 2, 8, 128) for y in swap_groups(parts)]
            for side in range(2):
                for h in range(2):
                    pair = jnp.concatenate([rows[2 * h][:, side], rows[2 * h + 1][:, side]], axis=1)
                    mats_ref[side, :, core, 16 * h : 16 * h + 16, 128 * t : 128 * t + 128] = (
                        pair.astype(BF16)
                    )
    left = mats_ref[0, :, me].reshape(256, 512)
    right = mats_ref[1].reshape(512, 512)
    tri = dot(left, right, (1, 1)).reshape(8, 4, 8, 512)
    for t in range(4):
        parts = [tri[:, a, :, 128 * t : 128 * t + 128].reshape(64, 128) for a in range(4)]
        cols = [x.reshape(8, 8, 128) for x in swap_groups(parts)]
        for h in range(2):
            tri_ref[:, 2 * t + h] = jnp.concatenate(
                [cols[2 * h], cols[2 * h + 1]], axis=1
            ).astype(BF16)


def output_kernel(
    tri_ref, nt_ref, og_ref, w_ref, wo_ref, gain_ref, bias_ref, tg_ref, gg_ref, ol_ref, scr
):
    gain, bias = column(gain_ref), column(bias_ref)
    scr[...] = tri_ref[...].astype(F32).reshape(1024, 128)
    total = None
    for n in range(4):
        lanes = slice(256 * n, 256 * n + 256)
        unit, rstd = norm_unit(load_strided(scr, n, 0, 8))
        tri = (unit * gain + bias).astype(BF16)
        projected = dot(wo_ref[...], tri, (0, 0))
        gate = jax.nn.sigmoid(dot(w_ref[:, 512:640], nt_ref[:, lanes], (0, 0)))
        cotangent = load_t(og_ref, n)
        scaled = (cotangent * gate).astype(BF16)
        gg_ref[:, lanes] = (cotangent * projected * gate * (1.0 - gate)).astype(BF16)
        local = dot(tri, scaled, (1, 1))
        total = local if total is None else total + local
        back = dot(wo_ref[...], scaled, (1, 0))
        store_strided(scr, n, 0, 8, norm_backward(back, unit, rstd, gain))
    ol_ref[...] = total
    tg_ref[...] = scr[...].reshape(64, 16, 128).astype(BF16)


def triangle_back_kernel(own_ref, other_ref, mats_ref, out_ref, tg, rg):
    me = lax.axis_index("core")
    for ref, core in ((own_ref, me), (other_ref, 1 - me)):
        for t in range(4):
            parts = []
            for h in range(2):
                both = ref[:, 2 * t + h].astype(F32)
                parts += [both[:, :8].reshape(64, 128), both[:, 8:].reshape(64, 128)]
            rows = [y.reshape(8, 8, 128) for y in swap_groups(parts)]
            for h in range(2):
                tg[:, core, 16 * h : 16 * h + 16, 128 * t : 128 * t + 128] = jnp.concatenate(
                    [rows[2 * h], rows[2 * h + 1]], axis=1
                ).astype(BF16)
    right = mats_ref[1].reshape(512, 512)
    left_grad = dot(tg[:, me].reshape(256, 512), right, (1, 0)).reshape(8, 4, 8, 512)
    left = mats_ref[0].reshape(512, 512)
    rg[...] = dot(tg[...].reshape(512, 512), left, (0, 0)).reshape(8, 2, 32, 512)
    right_grad = rg[:, me].reshape(8, 4, 8, 512)
    for t in range(4):
        cols = []
        for grad in (left_grad, right_grad):
            parts = [grad[:, a, :, 128 * t : 128 * t + 128].reshape(64, 128) for a in range(4)]
            cols.append([x.reshape(8, 8, 128) for x in swap_groups(parts)])
        for f in range(4):
            out_ref[:, 4 * t + f] = jnp.concatenate([cols[0][f], cols[1][f]], axis=1).astype(BF16)


def input_kernel(
    valid_ref, grads_ref, gg_ref, xt_ref, w_ref, gain_ref, bias_ref, gp_ref, il_ref, scr
):
    gain, bias = column(gain_ref), column(bias_ref)
    scr[...] = grads_ref[...].astype(F32).reshape(2048, 128)
    total = None
    for n in range(4):
        lanes = slice(256 * n, 256 * n + 256)
        unit, rstd = norm_unit(xt_ref[:, lanes].astype(F32))
        normed = (unit * gain + bias).astype(BF16)
        proj = dot(w_ref[:, :512], normed, (0, 0))
        mask = pair_mask(valid_ref[0], n)
        pieces = []
        for side in range(2):
            val = proj[256 * side : 256 * side + 128]
            sig = jax.nn.sigmoid(proj[256 * side + 128 : 256 * side + 256])
            grad = load_strided(scr, n, 8 * side, 16) * mask * sig
            pieces += [grad.astype(BF16), (grad * val * (1.0 - sig)).astype(BF16)]
        pieces.append(gg_ref[:, lanes])
        proj_grad = jnp.concatenate(pieces, axis=0)
        local = dot(normed, proj_grad, (1, 1))
        total = local if total is None else total + local
        back = dot(w_ref[...], proj_grad, (1, 0))
        grad = norm_backward(back, unit, rstd, gain)
        for d in range(2):
            gp_ref[:, 2 * n + d] = (
                grad[:, 128 * d : 128 * d + 128].T.astype(BF16).reshape(4, 32, 128)
            )
    for b in range(5):
        il_ref[b] = total[:, 128 * b : 128 * b + 128]


def call(kernel, outs, specs, scratch=()):
    return pl.pallas_call(
        kernel,
        out_shape=[jax.ShapeDtypeStruct(s, d) for s, d in outs],
        in_specs=specs,
        out_specs=[VMEM] * len(outs),
        scratch_shapes=[pltpu.VMEM(s, d) for s, d in scratch],
        compiler_params=pltpu.CompilerParams(vmem_limit_bytes=48 * 1024 * 1024),
    )


def spread(block, axes, n):
    return lax.all_to_all(jnp.broadcast_to(block[None], (n,) + block.shape), axes, 0, 0, tiled=True)


def sum_everywhere(values):
    mine = lax.all_to_all(values.astype(BF16).reshape(16, 48, 128), ROW, 0, 0, tiled=True)
    mine = jnp.sum(mine.astype(F32), axis=0).astype(BF16)
    mine = jnp.sum(spread(mine, "col", 16).astype(F32), axis=0).astype(BF16)
    return spread(mine, ROW, 16).reshape(768, 128).astype(F32)


def other_core(x):
    return lax.ppermute(x, "core", [(0, 1), (1, 0)])


def shards(pair_act, out_grad, valid_count, w_in, w_out, in_gain, in_bias, out_gain, out_bias):
    gains = [g.reshape(1, 128) for g in (in_gain, in_bias, out_gain, out_bias)]
    x_t, normed_t, lr = call(
        project_kernel,
        [((128, 1024), BF16), ((128, 1024), BF16), ((128, 16, 128), BF16)],
        [SMEM] + [VMEM] * 4,
        [((2048, 128), F32)],
    )(valid_count, pair_act.reshape(4, 8, 32, 128), w_in, gains[0], gains[1])
    own = lax.all_to_all(lr, CHIPS, 0, 0, tiled=True)
    other = other_core(own)
    mats, tri = call(
        triangle_kernel,
        [((2, 8, 2, 32, 512), BF16), ((8, 8, 16, 128), BF16)],
        [VMEM] * 2,
    )(own.reshape(8, 16, 16, 128), other.reshape(8, 16, 16, 128))
    tri = lax.all_to_all(tri.reshape(128, 8, 128), CHIPS, 0, 0, tiled=True)
    tri_grad, gate_grad, out_local = call(
        output_kernel,
        [((64, 16, 128), BF16), ((128, 1024), BF16), ((128, 128), F32)],
        [VMEM] * 7,
        [((1024, 128), F32)],
    )(
        tri.reshape(64, 16, 128),
        normed_t,
        out_grad.reshape(4, 8, 32, 128),
        w_in,
        w_out,
        gains[2],
        gains[3],
    )
    own = lax.all_to_all(tri_grad.reshape(128, 8, 128), CHIPS, 0, 0, tiled=True)
    other = other_core(own)
    (grads,) = call(
        triangle_back_kernel,
        [((8, 16, 16, 128), BF16)],
        [VMEM] * 3,
        [((8, 2, 32, 512), BF16), ((8, 2, 32, 512), F32)],
    )(own.reshape(8, 8, 16, 128), other.reshape(8, 8, 16, 128), mats)
    grads = lax.all_to_all(grads.reshape(128, 16, 128), CHIPS, 0, 0, tiled=True)
    grad_pair, in_local = call(
        input_kernel,
        [((4, 8, 32, 128), BF16), ((5, 128, 128), F32)],
        [SMEM] + [VMEM] * 6,
        [((2048, 128), F32)],
    )(valid_count, grads, gate_grad, x_t, w_in, gains[0], gains[1])
    local = jnp.concatenate([in_local.reshape(640, 128), out_local], axis=0)
    total = sum_everywhere(local) * (1.0 / 512)
    grad_in = jnp.swapaxes(total[:640].reshape(5, 128, 128), 0, 1).reshape(128, 640)
    return grad_pair.reshape(32, 32, 128), grad_in, total[640:]


def solution(mesh):
    fine = Mesh(mesh.devices.reshape(8, 2, 16), ("rh", "core", "col"))
    pairs = P(ROW, "col", None)
    return jax.shard_map(
        shards,
        mesh=fine,
        in_specs=(pairs, pairs, P(), P(), P(), P(), P(), P(), P()),
        out_specs=(pairs, P(), P()),
        check_vma=False,
    )
```

```python
import jax
import jax.numpy as jnp
from jax import lax
from jax.experimental import pallas as pl
from jax.experimental.pallas import tpu as pltpu
from jax.sharding import Mesh
from jax.sharding import PartitionSpec as P

EPS = 1e-05
F32 = jnp.float32
BF16 = jnp.bfloat16
ROW = ("yl", "x", "core")
COL = ("z", "yh")
CHIPS = ("x", "yl", "yh", "z")
VMEM = pl.BlockSpec(memory_space=pltpu.VMEM)
SMEM = pl.BlockSpec(memory_space=pltpu.SMEM)
HBM = pl.BlockSpec(memory_space=pltpu.HBM)
ANY = pl.BlockSpec(memory_space=pl.ANY)


def column(ref):
    wide = jnp.broadcast_to(ref[...], (128, 128)).T
    return jnp.concatenate([wide, wide], axis=1)


def dot(a, b, dims):
    return lax.dot_general(a, b, ((dims[:1], dims[1:]), ((), ())), preferred_element_type=F32)


def norm_unit(values):
    mean = jnp.sum(values, axis=0, keepdims=True) * (1.0 / 128)
    centred = values - mean
    var = jnp.sum(centred * centred, axis=0, keepdims=True) * (1.0 / 128)
    rstd = lax.rsqrt(var + EPS)
    return centred * rstd, rstd


def norm_backward(grad, unit, rstd, gain):
    scaled = grad * gain
    first = jnp.sum(scaled, axis=0, keepdims=True) * (1.0 / 128)
    second = jnp.sum(scaled * unit, axis=0, keepdims=True) * (1.0 / 128)
    return rstd * (scaled - first - unit * second)


def pair_mask(valid, n):
    lane = lax.broadcasted_iota(jnp.int32, (1, 256), 1)
    first = 8 * ((lane // 32) % 4) + 2 * n + lane // 128
    row_block = 8 * lax.axis_index("yl") + 2 * lax.axis_index("x") + lax.axis_index("core")
    col_block = 2 * lax.axis_index("z") + lax.axis_index("yh")
    return ((32 * row_block + first < valid) & (32 * col_block + lane % 32 < valid)).astype(F32)


def lanes_of(n):
    return slice(256 * n, 256 * n + 256)


def load_t(ref, n):
    return jnp.concatenate(
        [ref[:, q].reshape(128, 128).astype(F32).T for q in (2 * n, 2 * n + 1)], axis=1
    )


def load_strided(ref, n, first, stride):
    return jnp.concatenate(
        [ref[pl.ds(first + q, 128, stride=stride), :] for q in (2 * n, 2 * n + 1)], axis=1
    )


def store_strided(ref, n, first, stride, values):
    for d in range(2):
        ref[pl.ds(first + 2 * n + d, 128, stride=stride), :] = values[:, 128 * d : 128 * d + 128]


def swap_groups(parts):
    lane = lax.broadcasted_iota(jnp.int32, parts[0].shape, 1)
    low, even = lane < 64, lane % 64 < 32
    mid = [None] * 4
    for f in range(2):
        x, y = parts[f], parts[f + 2]
        mid[f] = jnp.where(low, x, pltpu.roll(y, 64, 1))
        mid[f + 2] = jnp.where(low, pltpu.roll(x, 64, 1), y)
    out = [None] * 4
    for f in (0, 2):
        x, y = mid[f], mid[f + 1]
        out[f] = jnp.where(even, x, pltpu.roll(y, 32, 1))
        out[f + 1] = jnp.where(even, pltpu.roll(x, 96, 1), y)
    return out


def left_right_kernel(
    valid_ref, x_hbm, w_hbm, gain_hbm, bias_hbm, og_hbm, wo_hbm,
    nt_ref, lr_ref, w_ref, og_ref, wo_ref, x_ref, gain_ref, bias_ref, scr, sem,
):
    pairs = (
        (gain_hbm, gain_ref), (bias_hbm, bias_ref), (x_hbm, x_ref), (w_hbm, w_ref),
        (og_hbm, og_ref), (wo_hbm, wo_ref),
    )
    copies = [pltpu.make_async_copy(src, dst, sem.at[i]) for i, (src, dst) in enumerate(pairs)]
    for copy in copies:
        copy.start()
    for copy in copies[:4]:
        copy.wait()
    gain, bias = column(gain_ref), column(bias_ref)
    for n in range(4):
        x = load_t(x_ref, n)
        unit, _ = norm_unit(x)
        normed = (unit * gain + bias).astype(BF16)
        nt_ref[:, lanes_of(n)] = normed
        proj = dot(w_ref[:, :512], normed, (0, 0))
        mask = pair_mask(valid_ref[0], n)
        left = jax.nn.sigmoid(proj[128:256]) * proj[:128] * mask
        right = jax.nn.sigmoid(proj[384:512]) * proj[256:384] * mask
        store_strided(scr, n, 0, 16, left)
        store_strided(scr, n, 8, 16, right)
    lr_ref[...] = scr[...].reshape(128, 16, 128).astype(BF16)
    for copy in copies[4:]:
        copy.wait()


def prepare_kernel(
    valid_ref, nt_ref, og_ref, w_ref, wo_ref, _, coef_ref, back_ref, scaled_ref, gate_ref
):
    for n in range(4):
        lanes = lanes_of(n)
        proj = dot(w_ref[...], nt_ref[:, lanes], (0, 0))
        mask = pair_mask(valid_ref[0], n)
        for side in range(2):
            val = proj[256 * side : 256 * side + 128]
            sig = jax.nn.sigmoid(proj[256 * side + 128 : 256 * side + 256])
            coef_ref[2 * side, :, lanes] = sig * mask
            coef_ref[2 * side + 1, :, lanes] = val * sig * (1.0 - sig) * mask
        gate = jax.nn.sigmoid(proj[512:])
        cotangent = load_t(og_ref, n)
        scaled = (cotangent * gate).astype(BF16)
        scaled_ref[:, lanes] = scaled
        back_ref[:, lanes] = dot(wo_ref[...], scaled, (1, 0))
        gate_ref[:, lanes] = cotangent * gate * (1.0 - gate)


def assemble(parts, store):
    rows = [y.reshape(8, 8, 128) for y in swap_groups(parts)]
    for h in range(2):
        pair = jnp.concatenate([rows[2 * h], rows[2 * h + 1]], axis=1).astype(BF16)
        store(slice(16 * h, 16 * h + 16), pair.reshape(2, 4, 16, 128))


def disassemble(matrix, t):
    parts = [matrix[:, a, :, 128 * t : 128 * t + 128].reshape(64, 128) for a in range(4)]
    return [x.reshape(8, 8, 128) for x in swap_groups(parts)]


def by_yl(ref, f):
    both = ref[f].astype(F32)
    return jnp.concatenate([both[:, 0], both[:, 1]], axis=0)


def assemble_sides(ref, out):
    for t in range(4):
        both = [by_yl(ref, (slice(None), slice(None), f % 2, 2 * t + f // 2)) for f in range(4)]
        for side in range(2):
            parts = [b[:, 8 * side : 8 * side + 8].reshape(64, 128) for b in both]

            def store(rows, values, side=side, t=t):
                out(side, rows, slice(128 * t, 128 * t + 128), values)

            assemble(parts, store)


def triangle_kernel(own_ref, other_ref, _, mats_ref, tri_ref):
    me = lax.axis_index("core")
    for ref, core in ((own_ref, me), (other_ref, 1 - me)):

        def out(side, rows, lanes, values, core=core):
            mats_ref[side, :, :, core, rows, lanes] = values

        assemble_sides(ref, out)
    left = mats_ref[0, :, :, me].reshape(256, 512)
    right = mats_ref[1].reshape(512, 512)
    tri = dot(left, right, (1, 1)).reshape(8, 4, 8, 512)
    for t in range(4):
        cols = disassemble(tri, t)
        for yh in range(2):
            pair = jnp.concatenate([cols[yh], cols[yh + 2]], axis=1).astype(BF16)
            for yl in range(2):
                tri_ref[:, yl, yh, t] = pair[4 * yl : 4 * yl + 4]


def output_kernel(tri_ref, back_ref, gain_ref, bias_ref, tg_ref, tri16_ref, scr):
    gain, bias = column(gain_ref), column(bias_ref)
    scr[...] = tri_ref[...].astype(F32).reshape(1024, 128)
    for n in range(4):
        unit, rstd = norm_unit(load_strided(scr, n, 0, 8))
        tri16_ref[:, lanes_of(n)] = (unit * gain + bias).astype(BF16)
        grad = norm_backward(back_ref[:, lanes_of(n)], unit, rstd, gain)
        store_strided(scr, n, 0, 8, grad)
    tg_ref[...] = scr[...].reshape(64, 16, 128).astype(BF16)


def gate_kernel(tri16_ref, scaled_ref, gate_ref, nt_ref, wo_ref, _, gg_ref, local_ref):
    projected = dot(wo_ref[...], tri16_ref[...], (0, 0))
    gg = (projected * gate_ref[...]).astype(BF16)
    gg_ref[...] = gg
    local_ref[0] = dot(nt_ref[...], gg, (1, 1))
    local_ref[1] = dot(tri16_ref[...], scaled_ref[...], (1, 1))


def assemble_grad(ref, out):
    for t in range(4):
        parts = [None] * 4
        for yh in range(2):
            both = by_yl(ref, (slice(None), slice(None), yh, t))
            parts[yh] = both[:, :8].reshape(64, 128)
            parts[yh + 2] = both[:, 8:].reshape(64, 128)

        def store(rows, values, t=t):
            out[:, :, rows, 128 * t : 128 * t + 128] = values

        assemble(parts, store)


def own_grads_kernel(own_ref, mats_ref, lg_ref, rg_ref, tg, full):
    me = lax.axis_index("core")
    assemble_grad(own_ref, tg)
    grad = tg[...].reshape(256, 512)
    left_grad = dot(grad, mats_ref[1].reshape(512, 512), (1, 0)).reshape(8, 4, 8, 512)
    for t in range(4):
        for f, block in enumerate(disassemble(left_grad, t)):
            lg_ref[t, f] = block
    left = mats_ref[0, :, :, me].reshape(256, 512)
    full[...] = dot(grad, left, (0, 0)).reshape(2, 4, 2, 32, 512)
    rg_ref[...] = full[:, :, me]


def grads_kernel(other_ref, lg_ref, rg_ref, mats_ref, _, out_ref, tg, full):
    me = lax.axis_index("core")
    assemble_grad(other_ref, tg)
    left = mats_ref[0, :, :, 1 - me].reshape(256, 512)
    full[...] = dot(tg[...].reshape(256, 512), left, (0, 0)).reshape(2, 4, 2, 32, 512)
    right_grad = (full[:, :, me] + rg_ref[...]).reshape(8, 4, 8, 512)
    for t in range(4):
        for f, block in enumerate(disassemble(right_grad, t)):
            both = jnp.concatenate([lg_ref[t, f], block], axis=1).astype(BF16)
            for yl in range(2):
                out_ref[:, yl, f % 2, 2 * t + f // 2] = both[4 * yl : 4 * yl + 4]


def weights_kernel(grads_ref, coef_ref, nt_ref, early_ref, pg_ref, local_ref, scr):
    scr[...] = grads_ref[...].astype(F32).reshape(2048, 128)
    total = None
    for n in range(4):
        lanes = lanes_of(n)
        for side in range(2):
            grad = load_strided(scr, n, 8 * side, 16)
            for part in (2 * side, 2 * side + 1):
                pg_ref[128 * part : 128 * part + 128, lanes] = (
                    grad * coef_ref[part, :, lanes]
                ).astype(BF16)
        local = dot(nt_ref[:, lanes], pg_ref[:, lanes], (1, 1))
        total = local if total is None else total + local
    for b in range(4):
        local_ref[128 * b : 128 * b + 128] = total[:, 128 * b : 128 * b + 128].astype(BF16)
    local_ref[512:] = early_ref[...].reshape(256, 128).astype(BF16)


def input_kernel(pg_ref, gg_ref, x_ref, w_ref, gain_ref, gp_ref):
    gain = column(gain_ref)
    for n in range(4):
        lanes = lanes_of(n)
        unit, rstd = norm_unit(load_t(x_ref, n))
        back = dot(w_ref[:, :512], pg_ref[:, lanes], (1, 0))
        back = back + dot(w_ref[:, 512:], gg_ref[:, lanes], (1, 0))
        grad = norm_backward(back, unit, rstd, gain)
        for d in range(2):
            gp_ref[:, 2 * n + d] = (
                grad[:, 128 * d : 128 * d + 128].T.astype(BF16).reshape(4, 32, 128)
            )


def sum_kernel(parts_ref, _, out_ref):
    total = jnp.sum(parts_ref[...].astype(F32), axis=0, keepdims=True).astype(BF16)
    out_ref[...] = jnp.broadcast_to(total, out_ref.shape)


def unpack_kernel(total_ref, in_ref, out_ref):
    for b in range(6):
        block = total_ref[128 * b : 128 * b + 128].astype(F32) * (1.0 / 512)
        if b < 5:
            in_ref[:, 128 * b : 128 * b + 128] = block
        else:
            out_ref[...] = block


def call(kernel, outs, specs, scratch=(), flops=0):
    size = sum(jnp.dtype(d).itemsize * elements(s) for s, d, *_ in outs)
    return pl.pallas_call(
        kernel,
        out_shape=[(where[0] if where else jax.ShapeDtypeStruct)(s, d) for s, d, *where in outs],
        in_specs=specs,
        out_specs=[VMEM] * len(outs),
        scratch_shapes=[pltpu.VMEM(*s) if isinstance(s, tuple) else s for s in scratch],
        compiler_params=pltpu.CompilerParams(vmem_limit_bytes=16 * 1024 * 1024),
        cost_estimate=pl.CostEstimate(flops=flops, bytes_accessed=2 * size, transcendentals=0),
    )


def elements(shape):
    size = 1
    for n in shape:
        size *= n
    return size


def in_hbm(x):
    return pltpu.with_memory_space_constraint(x, pltpu.HBM)


def exchange(x):
    return lax.all_to_all(x, CHIPS, 0, 0, tiled=True)


def other_core(x):
    return lax.ppermute(x, "core", [(0, 1), (1, 0)])


def exchange_16(x, axes):
    return lax.all_to_all(x, axes, 0, 0, tiled=True)


def add(parts, after):
    (out,) = call(sum_kernel, [((16, 48, 128), BF16)], [VMEM, HBM])(parts, in_hbm(after))
    return out


def shards(pair_act, out_grad, valid_count, w_in, w_out, in_gain, in_bias, out_gain, out_bias):
    in_gain, in_bias, out_gain, out_bias = (
        g.reshape(1, 128) for g in (in_gain, in_bias, out_gain, out_bias)
    )
    tall = (128, 1024)
    matrix = (2, 4, 32, 512)
    x = pair_act.reshape(4, 8, 32, 128)
    y = out_grad.reshape(4, 8, 32, 128)
    normed_t, lr, w_near, y_near, w_out_near = call(
        left_right_kernel,
        [
            (tall, BF16),
            ((128, 16, 128), BF16),
            ((128, 640), BF16, pltpu.VMEM),
            ((4, 8, 32, 128), BF16, pltpu.VMEM),
            ((128, 128), BF16, pltpu.VMEM),
        ],
        [SMEM] + [HBM] * 6,
        [
            ((4, 8, 32, 128), BF16),
            ((1, 128), F32),
            ((1, 128), F32),
            ((2048, 128), F32),
            pltpu.SemaphoreType.DMA((6,)),
        ],
        flops=134_000_000,
    )(valid_count, *(in_hbm(v) for v in (x, w_in, in_gain, in_bias, y, w_out)))
    own = exchange(lr).reshape(4, 2, 2, 8, 16, 128)
    other = other_core(own)
    coef, back, scaled, gate = call(
        prepare_kernel,
        [((4,) + tall, F32, pltpu.VMEM), (tall, F32), (tall, BF16), (tall, F32)],
        [SMEM] + [VMEM] * 4 + [ANY],
        flops=200_000_000,
    )(valid_count, normed_t, y_near, w_near, w_out_near, own)
    mats, tri = call(
        triangle_kernel,
        [((2, 2, 4, 2, 32, 512), BF16), ((4, 2, 2, 4, 16, 128), BF16)],
        [VMEM] * 2 + [ANY],
        flops=134_000_000,
    )(own, other, back)
    tri = exchange(tri.reshape(128, 8, 128))
    tri_grad, tri16 = call(
        output_kernel,
        [((64, 16, 128), BF16), (tall, BF16)],
        [VMEM] * 4,
        [((1024, 128), F32)],
    )(tri.reshape(64, 16, 128), back, out_gain, out_bias)
    own = exchange(tri_grad.reshape(128, 8, 128)).reshape(4, 2, 2, 4, 16, 128)
    other = other_core(own)
    gate_grad, early = call(
        gate_kernel,
        [(tall, BF16), ((2, 128, 128), F32)],
        [VMEM] * 5 + [ANY],
        flops=100_000_000,
    )(tri16, scaled, gate, normed_t, w_out, own)
    scratch = [(matrix, BF16), ((2, 4, 2, 32, 512), F32)]
    left_grad, right_grad = call(
        own_grads_kernel,
        [((4, 4, 8, 8, 128), F32), (matrix, F32)],
        [VMEM] * 2,
        scratch,
        flops=268_000_000,
    )(own, mats)
    (grads,) = call(
        grads_kernel,
        [((4, 2, 2, 8, 16, 128), BF16)],
        [VMEM] * 4 + [ANY],
        scratch,
        flops=134_000_000,
    )(other, left_grad, right_grad, mats, gate_grad)
    grads = exchange(grads.reshape(128, 16, 128))
    proj_grad, local = call(
        weights_kernel,
        [((512, 1024), BF16), ((768, 128), BF16)],
        [VMEM] * 4,
        [((2048, 128), F32)],
        flops=134_000_000,
    )(grads, coef, normed_t, early)
    parts = exchange_16(local.reshape(16, 48, 128), ROW)
    (grad_pair,) = call(
        input_kernel, [((4, 8, 32, 128), BF16, pltpu.HBM)], [VMEM] * 5, flops=168_000_000
    )(proj_grad, gate_grad, x, w_in, in_gain)
    parts = exchange_16(add(parts, grad_pair), ("yh", "z"))
    parts = exchange_16(add(parts, grad_pair), ROW)
    grad_in, grad_out = call(
        unpack_kernel, [((128, 640), F32), ((128, 128), F32)], [VMEM]
    )(parts.reshape(768, 128))
    return grad_pair.reshape(32, 32, 128), grad_in, grad_out


def solution(mesh):
    fine = Mesh(mesh.devices.reshape(2, 4, 2, 8, 2), ("yl", "x", "core", "z", "yh"))
    pairs = P(ROW, COL, None)
    return jax.shard_map(
        shards,
        mesh=fine,
        in_specs=(pairs, pairs, P(), P(), P(), P(), P(), P(), P()),
        out_specs=(pairs, P(), P()),
        check_vma=False,
    )
```

```python
import jax
import jax.numpy as jnp
from jax import lax
from jax.experimental import pallas as pl
from jax.experimental.pallas import tpu as pltpu
from jax.sharding import Mesh
from jax.sharding import PartitionSpec as P

EPS = 1e-05
F32 = jnp.float32
BF16 = jnp.bfloat16
ROW = ("yl", "x", "core")
COL = ("z", "yh")
CHIPS = ("x", "yl", "yh", "z")
VMEM = pl.BlockSpec(memory_space=pltpu.VMEM)
HBM = pl.BlockSpec(memory_space=pltpu.HBM)
ANY = pl.BlockSpec(memory_space=pl.ANY)


def column(ref):
    wide = jnp.broadcast_to(ref[...], (128, 128)).T
    return jnp.concatenate([wide, wide], axis=1)


def dot(a, b, dims):
    return lax.dot_general(a, b, ((dims[:1], dims[1:]), ((), ())), preferred_element_type=F32)


def norm_unit(values):
    mean = jnp.sum(values, axis=0, keepdims=True) * (1.0 / 128)
    centred = values - mean
    var = jnp.sum(centred * centred, axis=0, keepdims=True) * (1.0 / 128)
    rstd = lax.rsqrt(var + EPS)
    return centred * rstd, rstd


def norm_backward(grad, unit, rstd, gain):
    scaled = grad * gain
    first = jnp.sum(scaled, axis=0, keepdims=True) * (1.0 / 128)
    second = jnp.sum(scaled * unit, axis=0, keepdims=True) * (1.0 / 128)
    return rstd * (scaled - first - unit * second)


def pair_mask(valid, n):
    lane = lax.broadcasted_iota(jnp.int32, (1, 256), 1)
    first = 8 * ((lane // 32) % 4) + 2 * n + lane // 128
    row_block = 8 * lax.axis_index("yl") + 2 * lax.axis_index("x") + lax.axis_index("core")
    col_block = 2 * lax.axis_index("z") + lax.axis_index("yh")
    valid = jnp.broadcast_to(valid, (1, 256))
    return ((32 * row_block + first < valid) & (32 * col_block + lane % 32 < valid)).astype(F32)


def lanes_of(n):
    return slice(256 * n, 256 * n + 256)


def load_t(ref, n):
    return jnp.concatenate(
        [ref[:, q].reshape(128, 128).astype(F32).T for q in (2 * n, 2 * n + 1)], axis=1
    )


def load_strided(ref, n, first, stride):
    return jnp.concatenate(
        [ref[pl.ds(first + q, 128, stride=stride), :] for q in (2 * n, 2 * n + 1)], axis=1
    )


def store_strided(ref, n, first, stride, values):
    for d in range(2):
        ref[pl.ds(first + 2 * n + d, 128, stride=stride), :] = values[:, 128 * d : 128 * d + 128]


def swap_lanes(x, y, width):
    shape = x.shape
    x, y = x.reshape(128, 128), y.reshape(128, 128)
    first = lax.broadcasted_iota(jnp.int32, (128, 128), 1) % (2 * width) < width
    left = jnp.where(first, x, pltpu.roll(y, width, 1))
    right = jnp.where(first, pltpu.roll(x, 128 - width, 1), y)
    return left.reshape(shape), right.reshape(shape)


def swap_rows(x, y):
    return (
        jnp.concatenate([x[:, :8], y[:, :8]], axis=1),
        jnp.concatenate([x[:, 8:], y[:, 8:]], axis=1),
    )


def to_rows(x, y):
    return swap_lanes(*swap_rows(*swap_lanes(x, y, 32)), 64)


def to_blocks(x, y):
    return swap_lanes(*swap_rows(*swap_lanes(x, y, 64)), 32)


def left_right_kernel(
    x_hbm, w_hbm, gain_hbm, bias_hbm, og_hbm, wo_hbm,
    nt_ref, lr_ref, w_ref, og_ref, wo_ref,
    x_ref, gain_ref, bias_ref, scr, sem,
):
    pairs = (
        (x_hbm, x_ref), (w_hbm, w_ref), (gain_hbm, gain_ref), (bias_hbm, bias_ref),
        (og_hbm, og_ref), (wo_hbm, wo_ref),
    )
    copies = [pltpu.make_async_copy(src, dst, sem.at[i]) for i, (src, dst) in enumerate(pairs)]
    for copy in copies[:4]:
        copy.start()
    for copy in copies[:4]:
        copy.wait()
    for copy in copies[4:]:
        copy.start()
    gain, bias = column(gain_ref), column(bias_ref)
    for n in range(4):
        x = load_t(x_ref, n)
        unit, _ = norm_unit(x)
        normed = (unit * gain + bias).astype(BF16)
        nt_ref[:, lanes_of(n)] = normed
        proj = dot(w_ref[:, :512], normed, (0, 0))
        left = jax.nn.sigmoid(proj[128:256]) * proj[:128]
        right = jax.nn.sigmoid(proj[384:512]) * proj[256:384]
        store_strided(scr, n, 0, 16, left)
        store_strided(scr, n, 8, 16, right)
    lr_ref[...] = scr[...].reshape(128, 16, 128).astype(BF16)
    for copy in copies[4:]:
        copy.wait()


def prepare_kernel(
    valid_ref, nt_ref, og_ref, w_ref, wo_ref, _, coef_ref, back_ref, scaled_ref, gate_ref
):
    for n in range(4):
        lanes = lanes_of(n)
        proj = dot(w_ref[...], nt_ref[:, lanes], (0, 0))
        mask = pair_mask(valid_ref[...], n)
        for side in range(2):
            val = proj[256 * side : 256 * side + 128]
            sig = jax.nn.sigmoid(proj[256 * side + 128 : 256 * side + 256])
            coef_ref[2 * side, :, lanes] = sig * mask
            coef_ref[2 * side + 1, :, lanes] = val * sig * (1.0 - sig) * mask
        gate = jax.nn.sigmoid(proj[512:])
        cotangent = load_t(og_ref, n)
        scaled = (cotangent * gate).astype(BF16)
        scaled_ref[:, lanes] = scaled
        back_ref[:, lanes] = dot(wo_ref[...], scaled, (1, 0))
        gate_ref[:, lanes] = cotangent * gate * (1.0 - gate)


def lanes_t(t):
    return slice(128 * t, 128 * t + 128)


def by_yl(ref, yh, z):
    return jnp.concatenate([ref[:, 0, yh, z], ref[:, 1, yh, z]], axis=0)


def matrix_blocks(matrix, t):
    return to_blocks(matrix[:, :16, lanes_t(t)], matrix[:, 16:, lanes_t(t)])


def triangle_kernel(valid_ref, own_ref, other_ref, _, mats_ref, tri_ref):
    me = lax.axis_index("core")
    dims = (8, 16, 128)
    valid = jnp.broadcast_to(valid_ref[...].reshape(1, 1, 1), dims)
    block, row, lane = (lax.broadcasted_iota(jnp.int32, dims, d) for d in range(3))
    for ref, core in ((own_ref, me), (other_ref, 1 - me)):
        token = 64 * block + row + 32 * core
        for t in range(4):
            sides = [swap_rows(by_yl(ref, yh, 2 * t), by_yl(ref, yh, 2 * t + 1)) for yh in range(2)]
            for side in range(2):
                for h, values in enumerate(to_rows(sides[0][side], sides[1][side])):
                    keep = (token + 16 * h < valid) & (lane + 128 * t < valid)
                    mats_ref[side, :, :, core, 16 * h : 16 * h + 16, lanes_t(t)] = jnp.where(
                        keep, values, jnp.zeros_like(values)
                    ).reshape(2, 4, 16, 128)
    left = mats_ref[0, :, :, me].reshape(256, 512)
    right = mats_ref[1].reshape(512, 512)
    tri = dot(left, right, (1, 1)).astype(BF16).reshape(8, 32, 512)
    for t in range(4):
        for yh, block in enumerate(matrix_blocks(tri, t)):
            for yl in range(2):
                tri_ref[:, yl, yh, t] = block[4 * yl : 4 * yl + 4]


def output_kernel(tri_ref, back_ref, gain_ref, bias_ref, tg_ref, tri16_ref, scr):
    gain, bias = column(gain_ref), column(bias_ref)
    scr[...] = tri_ref[...].astype(F32).reshape(1024, 128)
    for n in range(4):
        unit, rstd = norm_unit(load_strided(scr, n, 0, 8))
        tri16_ref[:, lanes_of(n)] = (unit * gain + bias).astype(BF16)
        grad = norm_backward(back_ref[:, lanes_of(n)], unit, rstd, gain)
        store_strided(scr, n, 0, 8, grad)
    tg_ref[...] = scr[...].reshape(64, 16, 128).astype(BF16)


def gate_kernel(tri16_ref, scaled_ref, gate_ref, nt_ref, wo_ref, _, gg_ref, local_ref):
    projected = dot(wo_ref[...], tri16_ref[...], (0, 0))
    gg = (projected * gate_ref[...]).astype(BF16)
    gg_ref[...] = gg
    local_ref[0] = dot(nt_ref[...], gg, (1, 1))
    local_ref[1] = dot(tri16_ref[...], scaled_ref[...], (1, 1))


def assemble_grad(ref, out):
    for t in range(4):
        for h, values in enumerate(to_rows(by_yl(ref, 0, t), by_yl(ref, 1, t))):
            out[:, :, 16 * h : 16 * h + 16, lanes_t(t)] = values.reshape(2, 4, 16, 128)


def own_grads_kernel(own_ref, mats_ref, lg_ref, rg_ref, tg, full):
    me = lax.axis_index("core")
    assemble_grad(own_ref, tg)
    grad = tg[...].reshape(256, 512)
    left_grad = dot(grad, mats_ref[1].reshape(512, 512), (1, 0)).astype(BF16).reshape(8, 32, 512)
    for t in range(4):
        for yh, block in enumerate(matrix_blocks(left_grad, t)):
            lg_ref[t, yh] = block
    left = mats_ref[0, :, :, me].reshape(256, 512)
    full[...] = dot(grad, left, (0, 0)).reshape(2, 4, 2, 32, 512)
    rg_ref[...] = full[:, :, me]


def grads_kernel(other_ref, lg_ref, rg_ref, mats_ref, _, out_ref, tg, full):
    me = lax.axis_index("core")
    assemble_grad(other_ref, tg)
    left = mats_ref[0, :, :, 1 - me].reshape(256, 512)
    full[...] = dot(tg[...].reshape(256, 512), left, (0, 0)).reshape(2, 4, 2, 32, 512)
    right_grad = (full[:, :, me] + rg_ref[...]).astype(BF16).reshape(8, 32, 512)
    for t in range(4):
        for yh, block in enumerate(matrix_blocks(right_grad, t)):
            for z, both in enumerate(swap_rows(lg_ref[t, yh], block)):
                for yl in range(2):
                    out_ref[:, yl, yh, 2 * t + z] = both[4 * yl : 4 * yl + 4]


def proj_grad(scr, coef_ref, n):
    parts = []
    for side in range(2):
        grad = load_strided(scr, n, 8 * side, 16)
        for part in (2 * side, 2 * side + 1):
            parts.append((grad * coef_ref[part, :, lanes_of(n)]).astype(BF16))
    return jnp.concatenate(parts, axis=0)


def weights_kernel(grads_ref, coef_ref, nt_ref, early_ref, local_ref, scr):
    scr[...] = grads_ref[...].astype(F32).reshape(2048, 128)
    total = None
    for n in range(4):
        local = dot(nt_ref[:, lanes_of(n)], proj_grad(scr, coef_ref, n), (1, 1))
        total = local if total is None else total + local
    for b in range(4):
        local_ref[128 * b : 128 * b + 128] = total[:, 128 * b : 128 * b + 128].astype(BF16)
    local_ref[512:] = early_ref[...].reshape(256, 128).astype(BF16)


def input_kernel(grads_ref, coef_ref, gg_ref, x_ref, w_ref, gain_ref, gp_ref, scr):
    scr[...] = grads_ref[...].astype(F32).reshape(2048, 128)
    gain = column(gain_ref)
    for n in range(4):
        lanes = lanes_of(n)
        unit, rstd = norm_unit(load_t(x_ref, n))
        back = dot(w_ref[:, :512], proj_grad(scr, coef_ref, n), (1, 0))
        back = back + dot(w_ref[:, 512:], gg_ref[:, lanes], (1, 0))
        grad = norm_backward(back, unit, rstd, gain)
        for d in range(2):
            gp_ref[:, 2 * n + d] = (
                grad[:, 128 * d : 128 * d + 128].T.astype(BF16).reshape(4, 32, 128)
            )


def sum_kernel(parts_ref, _, out_ref):
    total = jnp.sum(parts_ref[...].astype(F32), axis=0, keepdims=True).astype(BF16)
    out_ref[...] = jnp.broadcast_to(total, out_ref.shape)


def unpack_kernel(total_ref, in_ref, out_ref):
    for b in range(6):
        block = total_ref[128 * b : 128 * b + 128].astype(F32) * (1.0 / 512)
        if b < 5:
            in_ref[:, 128 * b : 128 * b + 128] = block
        else:
            out_ref[...] = block


def call(kernel, outs, specs, scratch=(), flops=0):
    size = sum(jnp.dtype(d).itemsize * elements(s) for s, d, *_ in outs)
    return pl.pallas_call(
        kernel,
        out_shape=[(where[0] if where else jax.ShapeDtypeStruct)(s, d) for s, d, *where in outs],
        in_specs=specs,
        out_specs=[VMEM] * len(outs),
        scratch_shapes=[pltpu.VMEM(*s) if isinstance(s, tuple) else s for s in scratch],
        compiler_params=pltpu.CompilerParams(vmem_limit_bytes=16 * 1024 * 1024),
        cost_estimate=pl.CostEstimate(flops=flops, bytes_accessed=2 * size, transcendentals=0),
    )


def elements(shape):
    size = 1
    for n in shape:
        size *= n
    return size


def in_hbm(x):
    return pltpu.with_memory_space_constraint(x, pltpu.HBM)


def exchange(x):
    return lax.all_to_all(x, CHIPS, 0, 0, tiled=True)


def other_core(x):
    return lax.ppermute(x, "core", [(0, 1), (1, 0)])


def exchange_16(x, axes):
    return lax.all_to_all(x, axes, 0, 0, tiled=True)


def add(parts, after):
    (out,) = call(sum_kernel, [((16, 48, 128), BF16)], [VMEM, HBM])(parts, in_hbm(after))
    return out


def shards(pair_act, out_grad, valid_count, w_in, w_out, in_gain, in_bias, out_gain, out_bias):
    in_gain, in_bias, out_gain, out_bias = (
        g.reshape(1, 128) for g in (in_gain, in_bias, out_gain, out_bias)
    )
    tall = (128, 1024)
    matrix = (2, 4, 32, 512)
    valid = valid_count.reshape(1, 1)
    x = pair_act.reshape(4, 8, 32, 128)
    y = out_grad.reshape(4, 8, 32, 128)
    normed_t, lr, w_near, y_near, w_out_near = call(
        left_right_kernel,
        [
            (tall, BF16),
            ((128, 16, 128), BF16),
            ((128, 640), BF16, pltpu.VMEM),
            ((4, 8, 32, 128), BF16, pltpu.VMEM),
            ((128, 128), BF16, pltpu.VMEM),
        ],
        [HBM] * 6,
        [
            ((4, 8, 32, 128), BF16),
            ((1, 128), F32),
            ((1, 128), F32),
            ((2048, 128), F32),
            pltpu.SemaphoreType.DMA((6,)),
        ],
        flops=134_000_000,
    )(*(in_hbm(v) for v in (x, w_in, in_gain, in_bias, y, w_out)))
    own = exchange(lr).reshape(4, 2, 2, 8, 16, 128)
    other = other_core(own)
    coef, back, scaled, gate = call(
        prepare_kernel,
        [((4,) + tall, F32, pltpu.VMEM), (tall, F32), (tall, BF16), (tall, F32)],
        [VMEM] * 5 + [ANY],
        flops=200_000_000,
    )(valid, normed_t, y_near, w_near, w_out_near, own)
    mats, tri = call(
        triangle_kernel,
        [((2, 2, 4, 2, 32, 512), BF16), ((4, 2, 2, 4, 16, 128), BF16)],
        [VMEM] * 3 + [ANY],
        flops=134_000_000,
    )(valid, own, other, back)
    tri = exchange(tri.reshape(128, 8, 128))
    tri_grad, tri16 = call(
        output_kernel,
        [((64, 16, 128), BF16), (tall, BF16)],
        [VMEM] * 4,
        [((1024, 128), F32)],
    )(tri.reshape(64, 16, 128), back, out_gain, out_bias)
    own = exchange(tri_grad.reshape(128, 8, 128)).reshape(4, 2, 2, 4, 16, 128)
    other = other_core(own)
    gate_grad, early = call(
        gate_kernel,
        [(tall, BF16), ((2, 128, 128), F32)],
        [VMEM] * 5 + [ANY],
        flops=100_000_000,
    )(tri16, scaled, gate, normed_t, w_out, own)
    scratch = [(matrix, BF16), ((2, 4, 2, 32, 512), F32)]
    left_grad, right_grad = call(
        own_grads_kernel,
        [((4, 2, 8, 16, 128), BF16), (matrix, F32)],
        [VMEM] * 2,
        scratch,
        flops=268_000_000,
    )(own, mats)
    (grads,) = call(
        grads_kernel,
        [((4, 2, 2, 8, 16, 128), BF16)],
        [VMEM] * 4 + [ANY],
        scratch,
        flops=134_000_000,
    )(other, left_grad, right_grad, mats, gate_grad)
    grads = exchange(grads.reshape(128, 16, 128))
    (local,) = call(
        weights_kernel,
        [((768, 128), BF16)],
        [VMEM] * 4,
        [((2048, 128), F32)],
        flops=134_000_000,
    )(grads, coef, normed_t, early)
    parts = exchange_16(local.reshape(16, 48, 128), ROW)
    (grad_pair,) = call(
        input_kernel,
        [((4, 8, 32, 128), BF16, pltpu.HBM)],
        [VMEM] * 6,
        [((2048, 128), F32)],
        flops=168_000_000,
    )(grads, coef, gate_grad, x, w_in, in_gain)
    parts = exchange_16(add(parts, grad_pair), ("yh", "z"))
    parts = exchange_16(add(parts, grad_pair), ROW)
    grad_in, grad_out = call(
        unpack_kernel, [((128, 640), F32), ((128, 128), F32)], [VMEM]
    )(parts.reshape(768, 128))
    return grad_pair.reshape(32, 32, 128), grad_in, grad_out


def solution(mesh):
    fine = Mesh(mesh.devices.reshape(2, 4, 2, 8, 2), ("yl", "x", "core", "z", "yh"))
    pairs = P(ROW, COL, None)
    return jax.shard_map(
        shards,
        mesh=fine,
        in_specs=(pairs, pairs, P(), P(), P(), P(), P(), P(), P()),
        out_specs=(pairs, P(), P()),
        check_vma=False,
    )
```

```python
import jax
import jax.numpy as jnp
from jax import lax
from jax.experimental import pallas as pl
from jax.experimental.pallas import tpu as pltpu
from jax.sharding import Mesh
from jax.sharding import PartitionSpec as P

EPS = 1e-05
F32 = jnp.float32
BF16 = jnp.bfloat16
ROW = ("yl", "x", "core")
COL = ("z", "yh")
CHIPS = ("x", "yl", "yh", "z")
VMEM = pl.BlockSpec(memory_space=pltpu.VMEM)
HBM = pl.BlockSpec(memory_space=pltpu.HBM)
ROWS_16 = (2048 + 16, 128)
ROWS_8 = (1024 + 8, 128)
ANY = pl.BlockSpec(memory_space=pl.ANY)


def column(ref):
    wide = jnp.broadcast_to(ref[...], (128, 128)).T
    return jnp.concatenate([wide, wide], axis=1)


def dot(a, b, dims):
    return lax.dot_general(a, b, ((dims[:1], dims[1:]), ((), ())), preferred_element_type=F32)


def norm_unit(values):
    mean = jnp.sum(values, axis=0, keepdims=True) * (1.0 / 128)
    centred = values - mean
    var = jnp.sum(centred * centred, axis=0, keepdims=True) * (1.0 / 128)
    rstd = lax.rsqrt(var + EPS)
    return centred * rstd, rstd


def norm_backward(grad, unit, rstd, gain):
    scaled = grad * gain
    first = jnp.sum(scaled, axis=0, keepdims=True) * (1.0 / 128)
    second = jnp.sum(scaled * unit, axis=0, keepdims=True) * (1.0 / 128)
    return rstd * (scaled - first - unit * second)


def pair_mask(valid, n):
    lane = lax.broadcasted_iota(jnp.int32, (1, 256), 1)
    first = 8 * ((lane // 32) % 4) + 2 * n + lane // 128
    row_block = 8 * lax.axis_index("yl") + 2 * lax.axis_index("x") + lax.axis_index("core")
    col_block = 2 * lax.axis_index("z") + lax.axis_index("yh")
    valid = jnp.broadcast_to(valid, (1, 256))
    return ((32 * row_block + first < valid) & (32 * col_block + lane % 32 < valid)).astype(F32)


def lanes_of(n):
    return slice(256 * n, 256 * n + 256)


def load_t(ref, n):
    return jnp.concatenate(
        [ref[:, q].reshape(128, 128).T for q in (2 * n, 2 * n + 1)], axis=1
    ).astype(F32)


def load_strided(ref, n, first, stride):
    return jnp.concatenate(
        [ref[pl.ds(first + q, 128, stride=stride), :] for q in (2 * n, 2 * n + 1)], axis=1
    )


def store_strided(ref, n, first, stride, values):
    for d in range(2):
        ref[pl.ds(first + 2 * n + d, 128, stride=stride), :] = values[:, 128 * d : 128 * d + 128]


def swap_lanes(x, y, width):
    shape = x.shape
    x, y = x.reshape(128, 128), y.reshape(128, 128)
    first = lax.broadcasted_iota(jnp.int32, (128, 128), 1) % (2 * width) < width
    left = jnp.where(first, x, pltpu.roll(y, width, 1))
    right = jnp.where(first, pltpu.roll(x, 128 - width, 1), y)
    return left.reshape(shape), right.reshape(shape)


def swap_rows(x, y):
    return (
        jnp.concatenate([x[:, :8], y[:, :8]], axis=1),
        jnp.concatenate([x[:, 8:], y[:, 8:]], axis=1),
    )


def to_rows(x, y):
    return swap_lanes(*swap_rows(*swap_lanes(x, y, 32)), 64)


def to_blocks(x, y):
    return swap_lanes(*swap_rows(*swap_lanes(x, y, 64)), 32)


def left_right_kernel(
    x_hbm, w_hbm, gain_hbm, bias_hbm, og_hbm, wo_hbm,
    nt_ref, lr_ref, w_ref, og_ref, wo_ref,
    x_ref, gain_ref, bias_ref, scr, sem,
):
    pairs = (
        (x_hbm, x_ref), (w_hbm, w_ref), (gain_hbm, gain_ref), (bias_hbm, bias_ref),
        (og_hbm, og_ref), (wo_hbm, wo_ref),
    )
    copies = [pltpu.make_async_copy(src, dst, sem.at[i]) for i, (src, dst) in enumerate(pairs)]
    for copy in copies[:4]:
        copy.start()
    for copy in copies[:4]:
        copy.wait()
    for copy in copies[4:]:
        copy.start()
    gain, bias = column(gain_ref), column(bias_ref)
    weights = w_ref[:, :512].T
    for n in range(4):
        x = load_t(x_ref, n)
        unit, _ = norm_unit(x)
        normed = (unit * gain + bias).astype(BF16)
        nt_ref[:, lanes_of(n)] = normed
        proj = dot(weights, normed, (1, 0))
        left = jax.nn.sigmoid(proj[128:256]) * proj[:128]
        right = jax.nn.sigmoid(proj[384:512]) * proj[256:384]
        store_strided(scr, n, 0, 16, left)
        store_strided(scr, n, 8, 16, right)
    lr_ref[...] = scr[:2048].reshape(128, 16, 128).astype(BF16)
    for copy in copies[4:]:
        copy.wait()


def prepare_kernel(
    valid_ref, nt_ref, og_ref, w_ref, wo_ref, _, coef_ref, back_ref, scaled_ref, gate_ref
):
    weights = w_ref[...].T
    for n in range(4):
        lanes = lanes_of(n)
        proj = dot(weights, nt_ref[:, lanes], (1, 0))
        mask = pair_mask(valid_ref[...], n)
        for side in range(2):
            val = proj[256 * side : 256 * side + 128]
            sig = jax.nn.sigmoid(proj[256 * side + 128 : 256 * side + 256])
            coef_ref[2 * side, :, lanes] = sig * mask
            coef_ref[2 * side + 1, :, lanes] = val * sig * (1.0 - sig) * mask
        gate = jax.nn.sigmoid(proj[512:])
        cotangent = load_t(og_ref, n)
        scaled = (cotangent * gate).astype(BF16)
        scaled_ref[:, lanes] = scaled
        back_ref[:, lanes] = dot(wo_ref[...], scaled, (1, 0))
        gate_ref[:, lanes] = cotangent * gate * (1.0 - gate)


def lanes_t(t):
    return slice(128 * t, 128 * t + 128)


def by_yl(ref, yh, z):
    return jnp.concatenate([ref[:, 0, yh, z], ref[:, 1, yh, z]], axis=0)


def matrix_blocks(matrix, t):
    return to_blocks(matrix[:, :16, lanes_t(t)], matrix[:, 16:, lanes_t(t)])


def triangle_kernel(valid_ref, own_ref, other_ref, _, mats_ref, tri_ref):
    me = lax.axis_index("core")
    dims = (8, 16, 128)
    valid = jnp.broadcast_to(valid_ref[...].reshape(1, 1, 1), dims)
    block, row, lane = (lax.broadcasted_iota(jnp.int32, dims, d) for d in range(3))
    for ref, core in ((own_ref, me), (other_ref, 1 - me)):
        token = 64 * block + row + 32 * core
        for t in range(4):
            sides = [swap_rows(by_yl(ref, yh, 2 * t), by_yl(ref, yh, 2 * t + 1)) for yh in range(2)]
            for side in range(2):
                for h, values in enumerate(to_rows(sides[0][side], sides[1][side])):
                    keep = (token + 16 * h < valid) & (lane + 128 * t < valid)
                    mats_ref[side, :, :, core, 16 * h : 16 * h + 16, lanes_t(t)] = jnp.where(
                        keep, values, jnp.zeros_like(values)
                    ).reshape(2, 4, 16, 128)
    left = mats_ref[0, :, :, me].reshape(256, 512)
    right = mats_ref[1].reshape(512, 512)
    tri = dot(left, right, (1, 1)).astype(BF16).reshape(8, 32, 512)
    for t in range(4):
        for yh, block in enumerate(matrix_blocks(tri, t)):
            for yl in range(2):
                tri_ref[:, yl, yh, t] = block[4 * yl : 4 * yl + 4]


def output_kernel(tri_ref, back_ref, gain_ref, bias_ref, tg_ref, tri16_ref, scr):
    gain, bias = column(gain_ref), column(bias_ref)
    scr[:1024] = tri_ref[...].astype(F32).reshape(1024, 128)
    for n in range(4):
        unit, rstd = norm_unit(load_strided(scr, n, 0, 8))
        tri16_ref[:, lanes_of(n)] = (unit * gain + bias).astype(BF16)
        grad = norm_backward(back_ref[:, lanes_of(n)], unit, rstd, gain)
        store_strided(scr, n, 0, 8, grad)
    tg_ref[...] = scr[:1024].reshape(64, 16, 128).astype(BF16)


def gate_kernel(tri16_ref, scaled_ref, gate_ref, nt_ref, wo_ref, _, gg_ref, local_ref):
    projected = dot(wo_ref[...], tri16_ref[...], (0, 0))
    gg = (projected * gate_ref[...]).astype(BF16)
    gg_ref[...] = gg
    local_ref[0] = dot(nt_ref[...], gg, (1, 1))
    local_ref[1] = dot(tri16_ref[...], scaled_ref[...], (1, 1))


def assemble_grad(ref, out):
    for t in range(4):
        for h, values in enumerate(to_rows(by_yl(ref, 0, t), by_yl(ref, 1, t))):
            out[:, :, 16 * h : 16 * h + 16, lanes_t(t)] = values.reshape(2, 4, 16, 128)


def own_grads_kernel(own_ref, mats_ref, lg_ref, rg_ref, tg, full):
    me = lax.axis_index("core")
    assemble_grad(own_ref, tg)
    grad = tg[...].reshape(256, 512)
    left_grad = dot(grad, mats_ref[1].reshape(512, 512), (1, 0)).astype(BF16).reshape(8, 32, 512)
    for t in range(4):
        for yh, block in enumerate(matrix_blocks(left_grad, t)):
            lg_ref[t, yh] = block
    left = mats_ref[0, :, :, me].reshape(256, 512)
    full[...] = dot(grad, left, (0, 0)).reshape(2, 4, 2, 32, 512)
    rg_ref[...] = full[:, :, me]


def grads_kernel(other_ref, lg_ref, rg_ref, mats_ref, _, out_ref, tg, full):
    me = lax.axis_index("core")
    assemble_grad(other_ref, tg)
    left = mats_ref[0, :, :, 1 - me].reshape(256, 512)
    full[...] = dot(tg[...].reshape(256, 512), left, (0, 0)).reshape(2, 4, 2, 32, 512)
    right_grad = (full[:, :, me] + rg_ref[...]).astype(BF16).reshape(8, 32, 512)
    for t in range(4):
        for yh, block in enumerate(matrix_blocks(right_grad, t)):
            for z, both in enumerate(swap_rows(lg_ref[t, yh], block)):
                for yl in range(2):
                    out_ref[:, yl, yh, 2 * t + z] = both[4 * yl : 4 * yl + 4]


def proj_grad(scr, coef_ref, n):
    parts = []
    for side in range(2):
        grad = load_strided(scr, n, 8 * side, 16)
        for part in (2 * side, 2 * side + 1):
            parts.append((grad * coef_ref[part, :, lanes_of(n)]).astype(BF16))
    return jnp.concatenate(parts, axis=0)


def weights_kernel(grads_ref, coef_ref, nt_ref, early_ref, mine_ref, theirs_ref, scr, full):
    scr[:2048] = grads_ref[...].astype(F32).reshape(2048, 128)
    total = None
    for n in range(4):
        local = dot(nt_ref[:, lanes_of(n)], proj_grad(scr, coef_ref, n), (1, 1))
        total = local if total is None else total + local
    for b in range(6):
        block = total[:, lanes_t(b)] if b < 4 else early_ref[b - 4]
        full[b // 3, 128 * (b % 3) : 128 * (b % 3) + 128] = block
    me = lax.axis_index("core")
    mine_ref[...] = full[me]
    theirs_ref[...] = full[1 - me].astype(BF16)


def add_cores_kernel(mine_ref, theirs_ref, _, out_ref):
    out_ref[...] = (mine_ref[...] + theirs_ref[...].astype(F32)).astype(BF16)


def input_kernel(grads_ref, coef_ref, gg_ref, x_ref, w_ref, gain_ref, _, gp_ref, scr):
    scr[:2048] = grads_ref[...].astype(F32).reshape(2048, 128)
    gain = column(gain_ref)
    for n in range(4):
        lanes = lanes_of(n)
        unit, rstd = norm_unit(load_t(x_ref, n))
        back = dot(w_ref[:, :512], proj_grad(scr, coef_ref, n), (1, 0))
        back = back + dot(w_ref[:, 512:], gg_ref[:, lanes], (1, 0))
        grad = norm_backward(back, unit, rstd, gain)
        for d in range(2):
            gp_ref[:, 2 * n + d] = (
                grad[:, 128 * d : 128 * d + 128].T.astype(BF16).reshape(4, 32, 128)
            )


def sum_kernel(parts_ref, out_ref):
    total = jnp.sum(parts_ref[...].astype(F32), axis=0, keepdims=True).astype(BF16)
    out_ref[...] = jnp.broadcast_to(total, out_ref.shape)


def unpack_kernel(total_ref, gp_ref, gp_hbm, in_hbm, out_hbm, in_ref, out_ref, sem):
    pairs = ((gp_ref, gp_hbm), (in_ref, in_hbm), (out_ref, out_hbm))
    copies = [pltpu.make_async_copy(src, dst, sem.at[i]) for i, (src, dst) in enumerate(pairs)]
    copies[0].start()
    for core in range(2):
        half = total_ref[:, core].astype(F32).reshape(384, 128) * (1.0 / 512)
        for i in range(3):
            b, block = 3 * core + i, half[128 * i : 128 * i + 128]
            if b < 5:
                in_ref[:, lanes_t(b)] = block
            else:
                out_ref[...] = block
    for copy in copies[1:]:
        copy.start()
    for copy in copies:
        copy.wait()


def call(kernel, outs, specs, scratch=(), flops=0, out_spec=VMEM):
    size = sum(jnp.dtype(d).itemsize * elements(s) for s, d, *_ in outs)
    return pl.pallas_call(
        kernel,
        out_shape=[(where[0] if where else jax.ShapeDtypeStruct)(s, d) for s, d, *where in outs],
        in_specs=specs,
        out_specs=[out_spec] * len(outs),
        scratch_shapes=[pltpu.VMEM(*s) if isinstance(s, tuple) else s for s in scratch],
        compiler_params=pltpu.CompilerParams(vmem_limit_bytes=16 * 1024 * 1024),
        cost_estimate=pl.CostEstimate(flops=flops, bytes_accessed=2 * size, transcendentals=0),
    )


def elements(shape):
    size = 1
    for n in shape:
        size *= n
    return size


def in_hbm(x):
    return pltpu.with_memory_space_constraint(x, pltpu.HBM)


def exchange(x):
    return lax.all_to_all(x, CHIPS, 0, 0, tiled=True)


def other_core(x):
    return lax.ppermute(x, "core", [(0, 1), (1, 0)])


def swap(x, axes):
    return lax.all_to_all(x, axes, 0, 0, tiled=True)


def add(parts):
    (out,) = call(sum_kernel, [((16, 48, 128), BF16)], [VMEM])(parts)
    return out


def shards(pair_act, out_grad, valid_count, w_in, w_out, in_gain, in_bias, out_gain, out_bias):
    in_gain, in_bias, out_gain, out_bias = (
        g.reshape(1, 128) for g in (in_gain, in_bias, out_gain, out_bias)
    )
    tall = (128, 1024)
    matrix = (2, 4, 32, 512)
    valid = valid_count.reshape(1, 1)
    x = pair_act.reshape(4, 8, 32, 128)
    y = out_grad.reshape(4, 8, 32, 128)
    normed_t, lr, w_near, y_near, w_out_near = call(
        left_right_kernel,
        [
            (tall, BF16),
            ((128, 16, 128), BF16),
            ((128, 640), BF16, pltpu.VMEM),
            ((4, 8, 32, 128), BF16, pltpu.VMEM),
            ((128, 128), BF16, pltpu.VMEM),
        ],
        [HBM] * 6,
        [
            ((4, 8, 32, 128), BF16),
            ((1, 128), F32),
            ((1, 128), F32),
            (ROWS_16, F32),
            pltpu.SemaphoreType.DMA((6,)),
        ],
        flops=134_000_000,
    )(*(in_hbm(v) for v in (x, w_in, in_gain, in_bias, y, w_out)))
    own = exchange(lr).reshape(4, 2, 2, 8, 16, 128)
    other = other_core(own)
    coef, back, scaled, gate = call(
        prepare_kernel,
        [((4,) + tall, F32, pltpu.VMEM), (tall, F32), (tall, BF16), (tall, F32)],
        [VMEM] * 5 + [ANY],
        flops=200_000_000,
    )(valid, normed_t, y_near, w_near, w_out_near, own)
    mats, tri = call(
        triangle_kernel,
        [((2, 2, 4, 2, 32, 512), BF16), ((4, 2, 2, 4, 16, 128), BF16)],
        [VMEM] * 3 + [ANY],
        flops=134_000_000,
    )(valid, own, other, back)
    tri = exchange(tri.reshape(128, 8, 128))
    tri_grad, tri16 = call(
        output_kernel,
        [((64, 16, 128), BF16), (tall, BF16)],
        [VMEM] * 4,
        [(ROWS_8, F32)],
    )(tri.reshape(64, 16, 128), back, out_gain, out_bias)
    own = exchange(tri_grad.reshape(128, 8, 128)).reshape(4, 2, 2, 4, 16, 128)
    other = other_core(own)
    gate_grad, early = call(
        gate_kernel,
        [(tall, BF16), ((2, 128, 128), F32)],
        [VMEM] * 5 + [ANY],
        flops=100_000_000,
    )(tri16, scaled, gate, normed_t, w_out, own)
    scratch = [(matrix, BF16), ((2, 4, 2, 32, 512), F32)]
    left_grad, right_grad = call(
        own_grads_kernel,
        [((4, 2, 8, 16, 128), BF16), (matrix, F32)],
        [VMEM] * 2,
        scratch,
        flops=268_000_000,
    )(own, mats)
    (grads,) = call(
        grads_kernel,
        [((4, 2, 2, 8, 16, 128), BF16)],
        [VMEM] * 4 + [ANY],
        scratch,
        flops=134_000_000,
    )(other, left_grad, right_grad, mats, gate_grad)
    grads = exchange(grads.reshape(128, 16, 128))
    mine, theirs = call(
        weights_kernel,
        [((384, 128), F32), ((384, 128), BF16)],
        [VMEM] * 4,
        [(ROWS_16, F32), ((2, 384, 128), F32)],
        flops=134_000_000,
    )(grads, coef, normed_t, early)
    received = other_core(theirs)
    (grad_pair,) = call(
        input_kernel,
        [((4, 8, 32, 128), BF16, pltpu.VMEM)],
        [VMEM] * 6 + [ANY],
        [(ROWS_16, F32)],
        flops=168_000_000,
    )(grads, coef, gate_grad, x, w_in, in_gain, theirs)
    (chip,) = call(add_cores_kernel, [((384, 128), BF16)], [VMEM, VMEM, ANY])(
        mine, received, grad_pair
    )
    parts = swap(chip.reshape(8, 48, 128), ("yl", "x"))
    parts = swap(add(parts), ("yh", "z"))
    parts = swap(add(parts), ROW)
    grad_pair, grad_in, grad_out = call(
        unpack_kernel,
        [
            ((4, 8, 32, 128), BF16, pltpu.HBM),
            ((128, 640), F32, pltpu.HBM),
            ((128, 128), F32, pltpu.HBM),
        ],
        [VMEM] * 2,
        [((128, 640), F32), ((128, 128), F32), pltpu.SemaphoreType.DMA((3,))],
        out_spec=HBM,
    )(parts.reshape(8, 2, 48, 128), grad_pair)
    return grad_pair.reshape(32, 32, 128), grad_in, grad_out


def solution(mesh):
    fine = Mesh(mesh.devices.reshape(2, 4, 2, 8, 2), ("yl", "x", "core", "z", "yh"))
    pairs = P(ROW, COL, None)
    return jax.shard_map(
        shards,
        mesh=fine,
        in_specs=(pairs, pairs, P(), P(), P(), P(), P(), P(), P()),
        out_specs=(pairs, P(), P()),
        check_vma=False,
    )
```

```python
import jax
import jax.numpy as jnp
from jax import lax
from jax.experimental import pallas as pl
from jax.experimental.pallas import tpu as pltpu
from jax.sharding import Mesh
from jax.sharding import PartitionSpec as P

EPS = 1e-05
F32 = jnp.float32
BF16 = jnp.bfloat16
ROW = ("yl", "x", "core")
COL = ("z", "yh")
CHIPS = ("x", "yl", "yh", "z")
VMEM = pl.BlockSpec(memory_space=pltpu.VMEM)
HBM = pl.BlockSpec(memory_space=pltpu.HBM)
ROWS_16 = (2048 + 16, 128)
ROWS_8 = (1024 + 8, 128)
ANY = pl.BlockSpec(memory_space=pl.ANY)


def column(ref):
    wide = jnp.broadcast_to(ref[...], (128, 128)).T
    return jnp.concatenate([wide, wide], axis=1)


def dot(a, b, dims):
    return lax.dot_general(a, b, ((dims[:1], dims[1:]), ((), ())), preferred_element_type=F32)


def norm_unit(values):
    mean = jnp.sum(values, axis=0, keepdims=True) * (1.0 / 128)
    centred = values - mean
    var = jnp.sum(centred * centred, axis=0, keepdims=True) * (1.0 / 128)
    rstd = lax.rsqrt(var + EPS)
    return centred * rstd, rstd


def norm_backward(grad, unit, rstd, gain):
    scaled = grad * gain
    first = jnp.sum(scaled, axis=0, keepdims=True) * (1.0 / 128)
    second = jnp.sum(scaled * unit, axis=0, keepdims=True) * (1.0 / 128)
    return rstd * (scaled - first - unit * second)


def pair_mask(valid, n):
    lane = lax.broadcasted_iota(jnp.int32, (1, 256), 1)
    first = 8 * ((lane // 32) % 4) + 2 * n + lane // 128
    row_block = 8 * lax.axis_index("yl") + 2 * lax.axis_index("x") + lax.axis_index("core")
    col_block = 2 * lax.axis_index("z") + lax.axis_index("yh")
    valid = jnp.broadcast_to(valid, (1, 256))
    return ((32 * row_block + first < valid) & (32 * col_block + lane % 32 < valid)).astype(F32)


def lanes_of(n):
    return slice(256 * n, 256 * n + 256)


def load_t(ref, n):
    return jnp.concatenate(
        [ref[:, q].reshape(128, 128).T for q in (2 * n, 2 * n + 1)], axis=1
    ).astype(F32)


def load_strided(ref, n, first, stride):
    return jnp.concatenate(
        [ref[pl.ds(first + q, 128, stride=stride), :] for q in (2 * n, 2 * n + 1)], axis=1
    )


def store_strided(ref, n, first, stride, values):
    for d in range(2):
        ref[pl.ds(first + 2 * n + d, 128, stride=stride), :] = values[:, 128 * d : 128 * d + 128]


def swap_lanes(x, y, width):
    shape = x.shape
    x, y = x.reshape(128, 128), y.reshape(128, 128)
    first = lax.broadcasted_iota(jnp.int32, (128, 128), 1) % (2 * width) < width
    left = jnp.where(first, x, pltpu.roll(y, width, 1))
    right = jnp.where(first, pltpu.roll(x, 128 - width, 1), y)
    return left.reshape(shape), right.reshape(shape)


def swap_rows(x, y):
    return (
        jnp.concatenate([x[:, :8], y[:, :8]], axis=1),
        jnp.concatenate([x[:, 8:], y[:, 8:]], axis=1),
    )


def to_rows(x, y):
    return swap_lanes(*swap_rows(*swap_lanes(x, y, 32)), 64)


def to_blocks(x, y):
    return swap_lanes(*swap_rows(*swap_lanes(x, y, 64)), 32)


def left_right_kernel(
    x_hbm, w_hbm, gain_hbm, bias_hbm, og_hbm, wo_hbm,
    nt_ref, lr_ref, w_ref, og_ref, wo_ref,
    x_ref, gain_ref, bias_ref, scr, sem,
):
    pairs = (
        (x_hbm, x_ref), (w_hbm, w_ref), (gain_hbm, gain_ref), (bias_hbm, bias_ref),
        (og_hbm, og_ref), (wo_hbm, wo_ref),
    )
    copies = [pltpu.make_async_copy(src, dst, sem.at[i]) for i, (src, dst) in enumerate(pairs)]
    for copy in copies[:4]:
        copy.start()
    for copy in copies[:4]:
        copy.wait()
    for copy in copies[4:]:
        copy.start()
    gain, bias = column(gain_ref), column(bias_ref)
    weights = w_ref[:, :512].T
    for n in range(4):
        x = load_t(x_ref, n)
        unit, _ = norm_unit(x)
        normed = (unit * gain + bias).astype(BF16)
        nt_ref[:, lanes_of(n)] = normed
        proj = dot(weights, normed, (1, 0))
        left = jax.nn.sigmoid(proj[128:256]) * proj[:128]
        right = jax.nn.sigmoid(proj[384:512]) * proj[256:384]
        store_strided(scr, n, 0, 16, left)
        store_strided(scr, n, 8, 16, right)
    lr_ref[...] = scr[:2048].reshape(128, 16, 128).astype(BF16)
    for copy in copies[4:]:
        copy.wait()


def prepare_kernel(
    valid_ref, nt_ref, og_ref, w_ref, wo_ref, _, coef_ref, back_ref, scaled_ref, gate_ref
):
    weights = w_ref[...].T
    for n in range(4):
        lanes = lanes_of(n)
        proj = dot(weights, nt_ref[:, lanes], (1, 0))
        mask = pair_mask(valid_ref[...], n)
        for side in range(2):
            val = proj[256 * side : 256 * side + 128]
            sig = jax.nn.sigmoid(proj[256 * side + 128 : 256 * side + 256])
            coef_ref[2 * side, :, lanes] = sig * mask
            coef_ref[2 * side + 1, :, lanes] = val * sig * (1.0 - sig) * mask
        gate = jax.nn.sigmoid(proj[512:])
        cotangent = load_t(og_ref, n)
        scaled = (cotangent * gate).astype(BF16)
        scaled_ref[:, lanes] = scaled
        back_ref[:, lanes] = dot(wo_ref[...], scaled, (1, 0))
        gate_ref[:, lanes] = cotangent * gate * (1.0 - gate)


def lanes_t(t):
    return slice(128 * t, 128 * t + 128)


def by_yl(ref, yh, z):
    return jnp.concatenate([ref[:, 0, yh, z], ref[:, 1, yh, z]], axis=0)


def matrix_blocks(matrix, t):
    return to_blocks(matrix[:, :16, lanes_t(t)], matrix[:, 16:, lanes_t(t)])


def assemble(ref, core, valid, outs):
    dims = (8, 16, 128)
    block, row, lane = (lax.broadcasted_iota(jnp.int32, dims, d) for d in range(3))
    token = 64 * block + row + 32 * core
    valid = jnp.broadcast_to(valid, dims)
    for t in range(4):
        sides = [swap_rows(by_yl(ref, yh, 2 * t), by_yl(ref, yh, 2 * t + 1)) for yh in range(2)]
        for side, out in outs:
            for h, values in enumerate(to_rows(sides[0][side], sides[1][side])):
                keep = (token + 16 * h < valid) & (lane + 128 * t < valid)
                values = jnp.where(keep, values, jnp.zeros_like(values))
                out(slice(16 * h, 16 * h + 16), lanes_t(t), values.reshape(2, 4, 16, 128))


def store_in(ref, core=None):
    def store(rows, lanes, values):
        if core is None:
            ref[:, :, rows, lanes] = values
        else:
            ref[:, :, core, rows, lanes] = values

    return store


def triangle_kernel(
    valid_ref, own_ref, other_ref, _, left_ref, right_ref, tri_ref, valid_near_ref
):
    me = lax.axis_index("core")
    valid = valid_ref[...].reshape(1, 1, 1)
    valid_near_ref[...] = jnp.broadcast_to(valid_ref[...], (8, 128))
    assemble(own_ref, me, valid, ((0, store_in(left_ref)), (1, store_in(right_ref, me))))
    assemble(other_ref, 1 - me, valid, ((1, store_in(right_ref, 1 - me)),))
    left = left_ref[...].reshape(256, 512)
    right = right_ref[...].reshape(512, 512)
    tri = dot(left, right, (1, 1)).astype(BF16).reshape(8, 32, 512)
    for t in range(4):
        for yh, block in enumerate(matrix_blocks(tri, t)):
            for yl in range(2):
                tri_ref[:, yl, yh, t] = block[4 * yl : 4 * yl + 4]


def output_kernel(tri_ref, back_ref, gain_ref, bias_ref, tg_ref, tri16_ref, scr):
    gain, bias = column(gain_ref), column(bias_ref)
    scr[:1024] = tri_ref[...].astype(F32).reshape(1024, 128)
    for n in range(4):
        unit, rstd = norm_unit(load_strided(scr, n, 0, 8))
        tri16_ref[:, lanes_of(n)] = (unit * gain + bias).astype(BF16)
        grad = norm_backward(back_ref[:, lanes_of(n)], unit, rstd, gain)
        store_strided(scr, n, 0, 8, grad)
    tg_ref[...] = scr[:1024].reshape(64, 16, 128).astype(BF16)


def gate_kernel(tri16_ref, scaled_ref, gate_ref, nt_ref, wo_ref, _, gg_ref, local_ref):
    projected = dot(wo_ref[...], tri16_ref[...], (0, 0))
    gg = (projected * gate_ref[...]).astype(BF16)
    gg_ref[...] = gg
    local_ref[0] = dot(nt_ref[...], gg, (1, 1))
    local_ref[1] = dot(tri16_ref[...], scaled_ref[...], (1, 1))


def assemble_grad(ref, out):
    for t in range(4):
        for h, values in enumerate(to_rows(by_yl(ref, 0, t), by_yl(ref, 1, t))):
            out[:, :, 16 * h : 16 * h + 16, lanes_t(t)] = values.reshape(2, 4, 16, 128)


def own_columns(tg, turned, me):
    turned[...] = tg[...].reshape(256, 512).T.reshape(2, 4, 2, 32, 256)
    return turned[:, :, me].reshape(256, 256)


def own_grads_kernel(
    own_ref, left_ref, right_ref, blocks_ref, valid_ref, lg_ref, rg_ref, rest_ref, tg, turned
):
    me = lax.axis_index("core")
    assemble_grad(own_ref, tg)
    grad = tg[...].reshape(256, 512)
    right = right_ref[...].reshape(512, 512)
    left_grad = dot(grad, right, (1, 0)).astype(BF16).reshape(8, 32, 512)
    for t in range(4):
        for yh, block in enumerate(matrix_blocks(left_grad, t)):
            lg_ref[t, yh] = block
    rg_ref[...] = dot(own_columns(tg, turned, me), left_ref[...].reshape(256, 512), (1, 0))
    valid = valid_ref[:1, :].reshape(1, 1, 128)
    assemble(blocks_ref, 1 - me, valid, ((0, store_in(rest_ref)),))


def grads_kernel(other_ref, lg_ref, rg_ref, rest_ref, _, out_ref, tg, turned):
    me = lax.axis_index("core")
    assemble_grad(other_ref, tg)
    right_grad = dot(own_columns(tg, turned, me), rest_ref[...].reshape(256, 512), (1, 0))
    right_grad = (right_grad + rg_ref[...]).astype(BF16).reshape(8, 32, 512)
    for t in range(4):
        for yh, block in enumerate(matrix_blocks(right_grad, t)):
            for z, both in enumerate(swap_rows(lg_ref[t, yh], block)):
                for yl in range(2):
                    out_ref[:, yl, yh, 2 * t + z] = both[4 * yl : 4 * yl + 4]


def proj_grad(scr, coef_ref, n):
    parts = []
    for side in range(2):
        grad = load_strided(scr, n, 8 * side, 16)
        for part in (2 * side, 2 * side + 1):
            parts.append((grad * coef_ref[part, :, lanes_of(n)]).astype(BF16))
    return jnp.concatenate(parts, axis=0)


def weights_kernel(grads_ref, coef_ref, nt_ref, early_ref, mine_ref, theirs_ref, scr, full):
    scr[:2048] = grads_ref[...].astype(F32).reshape(2048, 128)
    total = None
    for n in range(4):
        local = dot(nt_ref[:, lanes_of(n)], proj_grad(scr, coef_ref, n), (1, 1))
        total = local if total is None else total + local
    for b in range(6):
        block = total[:, lanes_t(b)] if b < 4 else early_ref[b - 4]
        full[b // 3, 128 * (b % 3) : 128 * (b % 3) + 128] = block
    me = lax.axis_index("core")
    mine_ref[...] = full[me]
    theirs_ref[...] = full[1 - me].astype(BF16)


def add_cores_kernel(mine_ref, theirs_ref, _, out_ref):
    out_ref[...] = (mine_ref[...] + theirs_ref[...].astype(F32)).astype(BF16)


def input_kernel(grads_ref, coef_ref, gg_ref, x_ref, w_ref, gain_ref, _, gp_ref, scr):
    scr[:2048] = grads_ref[...].astype(F32).reshape(2048, 128)
    gain = column(gain_ref)
    for n in range(4):
        lanes = lanes_of(n)
        unit, rstd = norm_unit(load_t(x_ref, n))
        back = dot(w_ref[:, :512], proj_grad(scr, coef_ref, n), (1, 0))
        back = back + dot(w_ref[:, 512:], gg_ref[:, lanes], (1, 0))
        grad = norm_backward(back, unit, rstd, gain)
        for d in range(2):
            gp_ref[:, 2 * n + d] = (
                grad[:, 128 * d : 128 * d + 128].T.astype(BF16).reshape(4, 32, 128)
            )


def sum_kernel(parts_ref, out_ref):
    total = jnp.sum(parts_ref[...].astype(F32), axis=0, keepdims=True).astype(BF16)
    out_ref[...] = jnp.broadcast_to(total, out_ref.shape)


def unpack_kernel(total_ref, gp_ref, gp_hbm, in_hbm, out_hbm, in_ref, out_ref, sem):
    pairs = ((gp_ref, gp_hbm), (in_ref, in_hbm), (out_ref, out_hbm))
    copies = [pltpu.make_async_copy(src, dst, sem.at[i]) for i, (src, dst) in enumerate(pairs)]
    copies[0].start()
    for core in range(2):
        half = total_ref[:, core].astype(F32).reshape(384, 128) * (1.0 / 512)
        for i in range(3):
            b, block = 3 * core + i, half[128 * i : 128 * i + 128]
            if b < 5:
                in_ref[:, lanes_t(b)] = block
            else:
                out_ref[...] = block
    for copy in copies[1:]:
        copy.start()
    for copy in copies:
        copy.wait()


def call(kernel, outs, specs, scratch=(), flops=0, out_spec=VMEM):
    size = sum(jnp.dtype(d).itemsize * elements(s) for s, d, *_ in outs)
    return pl.pallas_call(
        kernel,
        out_shape=[(where[0] if where else jax.ShapeDtypeStruct)(s, d) for s, d, *where in outs],
        in_specs=specs,
        out_specs=[out_spec] * len(outs),
        scratch_shapes=[pltpu.VMEM(*s) if isinstance(s, tuple) else s for s in scratch],
        compiler_params=pltpu.CompilerParams(vmem_limit_bytes=16 * 1024 * 1024),
        cost_estimate=pl.CostEstimate(flops=flops, bytes_accessed=2 * size, transcendentals=0),
    )


def elements(shape):
    size = 1
    for n in shape:
        size *= n
    return size


def in_hbm(x):
    return pltpu.with_memory_space_constraint(x, pltpu.HBM)


def exchange(x):
    return lax.all_to_all(x, CHIPS, 0, 0, tiled=True)


def other_core(x):
    return lax.ppermute(x, "core", [(0, 1), (1, 0)])


def swap(x, axes):
    return lax.all_to_all(x, axes, 0, 0, tiled=True)


def add(parts):
    (out,) = call(sum_kernel, [((16, 48, 128), BF16)], [VMEM])(parts)
    return out


def shards(pair_act, out_grad, valid_count, w_in, w_out, in_gain, in_bias, out_gain, out_bias):
    in_gain, in_bias, out_gain, out_bias = (
        g.reshape(1, 128) for g in (in_gain, in_bias, out_gain, out_bias)
    )
    tall = (128, 1024)
    matrix = (2, 4, 32, 512)
    valid = valid_count.reshape(1, 1)
    x = pair_act.reshape(4, 8, 32, 128)
    y = out_grad.reshape(4, 8, 32, 128)
    normed_t, lr, w_near, y_near, w_out_near = call(
        left_right_kernel,
        [
            (tall, BF16),
            ((128, 16, 128), BF16),
            ((128, 640), BF16, pltpu.VMEM),
            ((4, 8, 32, 128), BF16, pltpu.VMEM),
            ((128, 128), BF16, pltpu.VMEM),
        ],
        [HBM] * 6,
        [
            ((4, 8, 32, 128), BF16),
            ((1, 128), F32),
            ((1, 128), F32),
            (ROWS_16, F32),
            pltpu.SemaphoreType.DMA((6,)),
        ],
        flops=134_000_000,
    )(*(in_hbm(v) for v in (x, w_in, in_gain, in_bias, y, w_out)))
    own = exchange(lr).reshape(4, 2, 2, 8, 16, 128)
    other = other_core(own)
    coef, back, scaled, gate = call(
        prepare_kernel,
        [((4,) + tall, F32, pltpu.VMEM), (tall, F32), (tall, BF16), (tall, F32)],
        [VMEM] * 5 + [ANY],
        flops=200_000_000,
    )(valid, normed_t, y_near, w_near, w_out_near, own)
    blocks = other
    left, right, tri, valid = call(
        triangle_kernel,
        [
            (matrix, BF16),
            ((2, 4, 2, 32, 512), BF16),
            ((4, 2, 2, 4, 16, 128), BF16),
            ((8, 128), jnp.int32),
        ],
        [VMEM] * 3 + [ANY],
        flops=134_000_000,
    )(valid, own, other, back)
    tri = exchange(tri.reshape(128, 8, 128))
    tri_grad, tri16 = call(
        output_kernel,
        [((64, 16, 128), BF16), (tall, BF16)],
        [VMEM] * 4,
        [(ROWS_8, F32)],
    )(tri.reshape(64, 16, 128), back, out_gain, out_bias)
    own = exchange(tri_grad.reshape(128, 8, 128)).reshape(4, 2, 2, 4, 16, 128)
    other = other_core(own)
    gate_grad, early = call(
        gate_kernel,
        [(tall, BF16), ((2, 128, 128), F32)],
        [VMEM] * 5 + [ANY],
        flops=100_000_000,
    )(tri16, scaled, gate, normed_t, w_out, own)
    scratch = [(matrix, BF16), ((2, 4, 2, 32, 256), BF16)]
    left_grad, right_grad, rest = call(
        own_grads_kernel,
        [((4, 2, 8, 16, 128), BF16), ((256, 512), F32), (matrix, BF16)],
        [VMEM] * 5,
        scratch,
        flops=200_000_000,
    )(own, left, right, blocks, valid)
    (grads,) = call(
        grads_kernel,
        [((4, 2, 2, 8, 16, 128), BF16)],
        [VMEM] * 4 + [ANY],
        scratch,
        flops=134_000_000,
    )(other, left_grad, right_grad, rest, gate_grad)
    grads = exchange(grads.reshape(128, 16, 128))
    mine, theirs = call(
        weights_kernel,
        [((384, 128), F32), ((384, 128), BF16)],
        [VMEM] * 4,
        [(ROWS_16, F32), ((2, 384, 128), F32)],
        flops=134_000_000,
    )(grads, coef, normed_t, early)
    received = other_core(theirs)
    (grad_pair,) = call(
        input_kernel,
        [((4, 8, 32, 128), BF16, pltpu.VMEM)],
        [VMEM] * 6 + [ANY],
        [(ROWS_16, F32)],
        flops=168_000_000,
    )(grads, coef, gate_grad, x, w_in, in_gain, theirs)
    (chip,) = call(add_cores_kernel, [((384, 128), BF16)], [VMEM, VMEM, ANY])(
        mine, received, grad_pair
    )
    parts = swap(chip.reshape(8, 48, 128), ("yl", "x"))
    parts = swap(add(parts), ("yh", "z"))
    parts = swap(add(parts), ROW)
    grad_pair, grad_in, grad_out = call(
        unpack_kernel,
        [
            ((4, 8, 32, 128), BF16, pltpu.HBM),
            ((128, 640), F32, pltpu.HBM),
            ((128, 128), F32, pltpu.HBM),
        ],
        [VMEM] * 2,
        [((128, 640), F32), ((128, 128), F32), pltpu.SemaphoreType.DMA((3,))],
        out_spec=HBM,
    )(parts.reshape(8, 2, 48, 128), grad_pair)
    return grad_pair.reshape(32, 32, 128), grad_in, grad_out


def solution(mesh):
    fine = Mesh(mesh.devices.reshape(2, 4, 2, 8, 2), ("yl", "x", "core", "z", "yh"))
    pairs = P(ROW, COL, None)
    return jax.shard_map(
        shards,
        mesh=fine,
        in_specs=(pairs, pairs, P(), P(), P(), P(), P(), P(), P()),
        out_specs=(pairs, P(), P()),
        check_vma=False,
    )
```
